512 devices in a mesh: lat: 64 (over x, z), chan: 8 (over y, core).
Axes of the slice: x: 4, y: 4, z: 16, core: 2. Of those that a mesh axis runs over, the one named last changes fastest.
Arguments:
- grid_field: bfloat16 [512, 1024, 384], P('lat', 'chan'), may hold values from -6 to 6
- norm_gain: float32 [384], replicated, may hold values from 0.25 to 1.75
- degree_gain: float32 [512, 384], replicated, may hold values from 0.25 to 4
- channel_mix: bfloat16 [2, 384, 384], replicated, may hold values from -0.21875 to 0.21875
Outputs:
- block_out: bfloat16 [512, 1024, 384], P('lat', None, 'chan')
The draws below stay inside these ranges and needn't reach their ends.
All inputs are finite; a program needn't handle non-finite values.
Results may differ from the reference program's by a relative error of at most 0.02.
Values may be sent and summed in bfloat16 or wider, within the bound.
No kernel may reach another device: no remote copies, remote signals or barrier semaphores. Data moves between devices by JAX's collectives and lax.ppermute only.
A program may use at most 128 MiB of HBM per device.

```python
import math
import jax
import jax.numpy as jnp
from jax import lax

NLAT = 512
EMBED = 384
NLON = 1024
DEGREES = 512
MODES = 512
N_LAT = 64


def level_of(own_key, shape, shards, least, top_value):
    loudness, own = 1.0, jax.random.fold_in(own_key, 6)
    for axis_at, blocks in shards:
        steps = jnp.exp(jax.random.uniform(jax.random.fold_in(own, axis_at), (blocks,), jnp.float32, least / len(shards), top_value / len(shards)))
        loudness = loudness * jnp.repeat(steps, shape[axis_at] // blocks).reshape([-1 if axis == axis_at else 1 for axis in range(len(shape))])
    return loudness


def bell_draw(rng, dims, width, limit, pieces=(), kind=jnp.bfloat16):
    result = jax.random.normal(rng, dims, jnp.float32) * width
    if len(pieces) > 0:
        result = level_of(rng, dims, pieces, -0.22, 0.18) * result
    return jnp.clip(result, min=-limit, max=limit).astype(kind)


def setup_inputs(seed: int = 0) -> dict:
    key_list = jax.random.split(jax.random.key(seed), 5)
    grid_field = bell_draw(key_list[0], (NLAT, NLON, EMBED), 1.0, 6.0, ((0, 64), (1, 8)))
    norm_gain = jnp.clip(1.0 + 0.15 * jax.random.normal(key_list[1], (EMBED,), jnp.float32), 0.25, 1.75)
    degree_gain = jnp.clip(jnp.exp(jax.random.uniform(key_list[2], (DEGREES, EMBED), jnp.float32, math.log(0.25), math.log(4.0))), 0.25, 4.0)
    channel_mix = bell_draw(key_list[3], (2, EMBED, EMBED), (2 * EMBED) ** -0.5, 0.21875)
    return dict(grid_field=grid_field, norm_gain=norm_gain, degree_gain=degree_gain, channel_mix=channel_mix)


LGAMMA_HALF_THREE = 0.5 * math.log(math.pi) - math.log(2.0)

def grid_points():
    theta = math.pi * (jnp.arange(NLAT, dtype=jnp.float32) + 0.5) / NLAT
    cosines = jnp.cos(theta)
    harmonic = jnp.arange(1, NLAT // 2 + 1, dtype=jnp.float32)
    series = lax.optimization_barrier(jnp.sum(jnp.cos(2.0 * harmonic[None, :] * theta[:, None]) / (4.0 * harmonic * harmonic - 1.0), axis=1))
    weights = 2.0 / NLAT * (1.0 - 2.0 * series)
    return (cosines, weights)

def legendre(orders, cosines):
    order_col = orders[:, None]
    cos_row = cosines[None, :]
    log_sine = 0.5 * jnp.log(1.0 - cos_row * cos_row)
    log_start = -0.5 * math.log(2.0) + 0.5 * (lax.lgamma(order_col + 1.5) - LGAMMA_HALF_THREE - lax.lgamma(order_col + 1.0)) + order_col * log_sine
    first_factor = jnp.sqrt(2.0 * order_col + 3.0)

    def advance(recur_state, degree):
        prev_one, prev_two, log_scale = recur_state
        level = degree.astype(jnp.float32)
        denom = jnp.maximum(level * level - order_col * order_col, 1.0)
        coef_a = jnp.sqrt(jnp.maximum(4.0 * level * level - 1.0, 1.0) / denom)
        coef_b = jnp.sqrt(jnp.maximum((level - 1.0) * (level - 1.0) - order_col * order_col, 0.0) * (2.0 * level + 1.0) / (denom * jnp.maximum(2.0 * level - 3.0, 1.0)))
        general = coef_a * cos_row * prev_one - coef_b * prev_two
        current = jnp.where(level == order_col, 1.0, jnp.where(level == order_col + 1.0, first_factor * cos_row * prev_one, jnp.where(level > order_col + 1.0, general, 0.0)))
        log_scale = jnp.where(level == order_col, log_start, log_scale)
        values = current * jnp.exp(log_scale)
        oversize = jnp.abs(current) > 1000000000000.0
        factor = jnp.where(oversize, 2.0 ** (-40), 1.0)
        log_scale = log_scale + jnp.where(oversize, 40.0 * math.log(2.0), 0.0)
        return ((current * factor, prev_one * factor, log_scale), values)
    zeros = jnp.zeros((orders.shape[0], cosines.shape[0]), jnp.float32)
    final_state, values = lax.scan(advance, (zeros, zeros, zeros), jnp.arange(DEGREES, dtype=jnp.int32))
    return values

def pair_weight(channel_mix):
    real_part = channel_mix[0]
    imag_part = channel_mix[1]
    upper = jnp.concatenate([real_part, imag_part], axis=1)
    lower = jnp.concatenate([-imag_part, real_part], axis=1)
    return jnp.concatenate([upper, lower], axis=0)

def reference(grid_field, norm_gain, degree_gain, channel_mix):
    values = grid_field.astype(jnp.float32)
    mean_value = lax.optimization_barrier(jnp.mean(values, axis=2, keepdims=True))
    centered = values - mean_value
    variance = lax.optimization_barrier(jnp.mean(centered * centered, axis=2, keepdims=True))
    normed = (centered * lax.rsqrt(variance + 1e-05) * norm_gain).astype(jnp.bfloat16)
    spectrum_c = jnp.fft.rfft(normed.astype(jnp.float32), axis=1)[:, :MODES, :] / NLON
    spectrum = jnp.stack([jnp.real(spectrum_c), jnp.imag(spectrum_c)], axis=2).astype(jnp.bfloat16)
    cosines, weights = grid_points()
    block_size = NLAT // N_LAT
    block_count = MODES // block_size
    blocks = jnp.moveaxis(spectrum.reshape(NLAT, block_count, block_size, 2, EMBED), 1, 0)
    paired_weight = pair_weight(channel_mix)

    def one_block(inputs):
        block_index, block_spec = inputs
        orders = (block_index * block_size + jnp.arange(block_size, dtype=jnp.int32)).astype(jnp.float32)
        leg_values = legendre(orders, cosines)
        forward_table = (leg_values * weights).astype(jnp.bfloat16)
        inverse_table = leg_values.astype(jnp.bfloat16)
        coeffs = jnp.einsum('ljn,njrc->ljrc', forward_table.astype(jnp.float32), block_spec.astype(jnp.float32))
        scaled = (coeffs * degree_gain[:, None, None, :]).astype(jnp.bfloat16)
        mixed = jnp.dot(scaled.reshape(-1, 2 * EMBED), paired_weight, preferred_element_type=jnp.float32).astype(jnp.bfloat16)
        mixed = mixed.reshape(DEGREES, block_size, 2, EMBED)
        field = jnp.einsum('ljn,ljrc->njrc', inverse_table.astype(jnp.float32), mixed.astype(jnp.float32))
        return field.astype(jnp.bfloat16)
    fields = lax.map(one_block, (jnp.arange(block_count, dtype=jnp.int32), blocks))
    fields = jnp.moveaxis(fields, 0, 1).reshape(NLAT, MODES, 2, EMBED)
    complex_field = fields[:, :, 0, :].astype(jnp.float32) + 1j * fields[:, :, 1, :].astype(jnp.float32)
    padded = jnp.pad(complex_field, ((0, 0), (0, NLON // 2 + 1 - MODES), (0, 0)))
    restored = NLON * jnp.fft.irfft(padded, n=NLON, axis=1)
    return (values + restored).astype(jnp.bfloat16)
```

```python
import math

import jax
import jax.numpy as jnp
import numpy as np
from jax import lax
from jax.experimental import pallas as pl
from jax.experimental.pallas import tpu as pltpu
from jax.sharding import PartitionSpec as P

NLAT = 512
EMBED = 384
NLON = 1024
DEGREES = 512
MODES = 512
BLOCK = 8


def grid_points():
    theta = math.pi * (np.arange(NLAT, dtype=np.float64) + 0.5) / NLAT
    harmonic = np.arange(1, NLAT // 2 + 1, dtype=np.float64)
    series = np.sum(
        np.cos(2.0 * harmonic[None, :] * theta[:, None]) / (4.0 * harmonic * harmonic - 1.0),
        axis=1,
    )
    weights = 2.0 / NLAT * (1.0 - 2.0 * series)
    return theta, weights


def order_starts():
    return np.array(
        [
            0.5 * (math.lgamma(m + 1.5) - math.lgamma(1.5) - math.lgamma(m + 1.0) - math.log(2.0))
            / math.log(2.0)
            for m in range(MODES)
        ]
    )


def dft_tables():
    phase = np.arange(MODES)[:, None] * np.arange(NLON)[None, :] % NLON
    angle = 2.0 * math.pi / NLON * phase
    parts = np.stack([np.cos(angle), -np.sin(angle)], axis=1)
    factor = np.where(np.arange(MODES) == 0, 1.0, 2.0)[:, None, None]
    forward = (parts / NLON).reshape(2 * MODES, NLON)
    inverse = (parts * factor).reshape(2 * MODES, NLON)
    return forward.astype(jnp.bfloat16), inverse.astype(jnp.bfloat16)


def pair_weight(channel_mix):
    real_part = channel_mix[0]
    imag_part = channel_mix[1]
    upper = jnp.concatenate([real_part, imag_part], axis=1)
    lower = jnp.concatenate([-imag_part, real_part], axis=1)
    return jnp.concatenate([upper, lower], axis=0)


def legendre_kernel(coef_ref, rows_ref, forward_ref, inverse_ref):
    cos_row = rows_ref[0:1, :]
    start = rows_ref[1:2, :]
    exponent = rows_ref[2:3, :]
    weights = rows_ref[3:4, :]

    def block(index, state):
        one, two, power = state
        base = index * BLOCK
        rows = []
        for k in range(BLOCK):
            a = coef_ref[0, base + k]
            b = coef_ref[1, base + k]
            s = coef_ref[2, base + k]
            one, two = (a * cos_row) * one - b * two + s * start, one
            rows.append(one)
        values = jnp.concatenate(rows, axis=0) * jnp.exp2(power)
        here = pl.ds(pl.multiple_of(base, BLOCK), BLOCK)
        forward_ref[here, :] = values * weights
        inverse_ref[here, :] = values
        large = jnp.abs(one) > 1000.0
        factor = jnp.where(large, 2.0**-40, 1.0)
        power = power + jnp.where(large, 40.0, 0.0)
        return one * factor, two * factor, power

    zeros = jnp.zeros((1, NLAT), jnp.float32)
    lax.fori_loop(0, DEGREES // BLOCK, block, (zeros, zeros, exponent))


def legendre_tables(order):
    theta, weights = grid_points()
    cos_row = jnp.asarray(np.cos(theta), jnp.float32)
    log_sine = jnp.asarray(np.log2(np.sin(theta)), jnp.float32)
    starts = jnp.asarray(order_starts(), jnp.float32)
    start = lax.dynamic_slice_in_dim(starts, order, 1)[0]
    m = order.astype(jnp.float32)
    log_start = start + m * log_sine
    exponent = jnp.floor(log_start)
    mantissa = jnp.exp2(log_start - exponent)
    rows = jnp.stack([cos_row, mantissa, exponent, jnp.asarray(weights, jnp.float32)])
    level = jnp.arange(DEGREES, dtype=jnp.float32)
    denom = jnp.maximum(level * level - m * m, 1.0)
    above = level > m
    coef_a = jnp.where(above, jnp.sqrt(jnp.maximum(4.0 * level * level - 1.0, 1.0) / denom), 0.0)
    coef_b = jnp.sqrt(
        jnp.maximum((level - 1.0) * (level - 1.0) - m * m, 0.0)
        * (2.0 * level + 1.0)
        / (denom * jnp.maximum(2.0 * level - 3.0, 1.0))
    )
    coef_b = jnp.where(above, coef_b, 0.0)
    first = jnp.where(level == m, 1.0, 0.0)
    coefs = jnp.stack([coef_a, coef_b, first])
    shape = jax.ShapeDtypeStruct((DEGREES, NLAT), jnp.float32)
    return pl.pallas_call(
        legendre_kernel,
        out_shape=(shape, shape),
        in_specs=[
            pl.BlockSpec(memory_space=pltpu.SMEM),
            pl.BlockSpec(memory_space=pltpu.VMEM),
        ],
        out_specs=(
            pl.BlockSpec(memory_space=pltpu.VMEM),
            pl.BlockSpec(memory_space=pltpu.VMEM),
        ),
        cost_estimate=pl.CostEstimate(flops=40_000_000, bytes_accessed=2_000_000, transcendentals=32768),
        compiler_params=pltpu.CompilerParams(vmem_limit_bytes=16 * 1024 * 1024),
    )(coefs, rows)


def on_device(grid_field, norm_gain, degree_gain, channel_mix):
    both = ("lat", "chan")
    forward_dft, inverse_dft = dft_tables()
    own = lax.all_to_all(grid_field, "chan", split_axis=0, concat_axis=1, tiled=True)
    own = own.reshape(NLON, EMBED)
    values = own.astype(jnp.float32)
    mean_value = jnp.mean(values, axis=1, keepdims=True)
    centered = values - mean_value
    variance = jnp.mean(centered * centered, axis=1, keepdims=True)
    normed = (centered * lax.rsqrt(variance + 1e-05) * norm_gain).astype(jnp.bfloat16)
    spectrum = jnp.dot(forward_dft, normed, preferred_element_type=jnp.float32)
    spectrum = spectrum.astype(jnp.bfloat16).reshape(MODES, 2, EMBED)
    arrived = lax.all_to_all(spectrum, both, split_axis=0, concat_axis=0, tiled=True)
    forward_table, inverse_table = legendre_tables(lax.axis_index(both))
    forward_table = forward_table.astype(jnp.bfloat16)
    inverse_table = inverse_table.astype(jnp.bfloat16)
    coeffs = jnp.einsum("lj,jrc->lrc", forward_table, arrived, preferred_element_type=jnp.float32)
    scaled = (coeffs * degree_gain[:, None, :]).astype(jnp.bfloat16)
    mixed = jnp.dot(
        scaled.reshape(DEGREES, 2 * EMBED),
        pair_weight(channel_mix),
        preferred_element_type=jnp.float32,
    ).astype(jnp.bfloat16)
    field = jnp.einsum("lj,lk->jk", inverse_table, mixed, preferred_element_type=jnp.float32)
    field = field.astype(jnp.bfloat16).reshape(NLAT, 2, EMBED)
    returned = lax.all_to_all(field, both, split_axis=0, concat_axis=0, tiled=True)
    restored = jnp.einsum(
        "kn,kc->nc",
        inverse_dft,
        returned.reshape(2 * MODES, EMBED),
        preferred_element_type=jnp.float32,
    )
    block_out = (values + restored).astype(jnp.bfloat16)
    return lax.all_to_all(
        block_out.reshape(1, NLON, EMBED), "chan", split_axis=2, concat_axis=0, tiled=True
    )


def solution(mesh):
    return jax.shard_map(
        on_device,
        mesh=mesh,
        in_specs=(P("lat", "chan", None), P(), P(), P()),
        out_specs=P("lat", None, "chan"),
        check_vma=False,
    )
```

```python
import math

import jax
import jax.numpy as jnp
import numpy as np
from jax import lax
from jax.experimental import pallas as pl
from jax.experimental.pallas import tpu as pltpu
from jax.sharding import PartitionSpec as P

NLAT = 512
EMBED = 384
NLON = 1024
DEGREES = 512
MODES = 512
VMEM_LIMIT = 16 * 1024 * 1024


def grid_points():
    theta = math.pi * (np.arange(NLAT, dtype=np.float64) + 0.5) / NLAT
    harmonic = np.arange(1, NLAT // 2 + 1, dtype=np.float64)
    series = np.sum(
        np.cos(2.0 * harmonic[None, :] * theta[:, None]) / (4.0 * harmonic * harmonic - 1.0),
        axis=1,
    )
    weights = 2.0 / NLAT * (1.0 - 2.0 * series)
    return theta, weights


def order_starts():
    return np.array(
        [
            0.5 * (math.lgamma(m + 1.5) - math.lgamma(1.5) - math.lgamma(m + 1.0) - math.log(2.0))
            / math.log(2.0)
            for m in range(MODES)
        ]
    )


def dft_tables():
    phase = np.arange(MODES)[:, None] * np.arange(NLON)[None, :] % NLON
    angle = 2.0 * math.pi / NLON * phase
    parts = np.stack([np.cos(angle), -np.sin(angle)], axis=1)
    factor = np.where(np.arange(MODES) == 0, 1.0, 2.0)[:, None, None]
    forward = (parts / NLON).transpose(1, 0, 2).reshape(2 * MODES, NLON)
    inverse = (parts * factor).reshape(2 * MODES, NLON)
    return forward.astype(jnp.bfloat16), inverse.astype(jnp.bfloat16)


def pair_weight(channel_mix):
    real_part = channel_mix[0]
    imag_part = channel_mix[1]
    upper = jnp.concatenate([real_part, imag_part], axis=1)
    lower = jnp.concatenate([-imag_part, real_part], axis=1)
    return jnp.concatenate([upper, lower], axis=0)


def permuted_latitudes():
    high, a, low = np.meshgrid(np.arange(4), np.arange(8), np.arange(16), indexing="ij")
    return ((16 * high + low) * 8 + a).reshape(-1)


def transform_kernel(grid_ref, gain_ref, table_ref, out_ref, normed_ref, held_ref, wide_ref, sem):
    copy = pltpu.make_async_copy(table_ref, held_ref, sem)
    copy.start()
    gain = gain_ref[...]
    for piece in range(8):
        rows = slice(128 * piece, 128 * piece + 128)
        values = grid_ref[rows, :].astype(jnp.float32)
        mean_value = jnp.mean(values, axis=1, keepdims=True)
        centered = values - mean_value
        variance = jnp.mean(centered * centered, axis=1, keepdims=True)
        normed_ref[rows, :] = (centered * lax.rsqrt(variance + 1e-05) * gain).astype(jnp.bfloat16)
    copy.wait()
    for r in range(2):
        spectrum = jnp.dot(
            held_ref[512 * r : 512 * r + 512, :],
            normed_ref[...],
            preferred_element_type=jnp.float32,
        )
        for t in range(3):
            wide_ref[pl.ds(2 * t + r, 512, stride=6), :] = spectrum[:, 128 * t : 128 * t + 128]
    out_ref[...] = wide_ref[...].astype(jnp.bfloat16)


def transform(grid, gain, table):
    vmem = pl.BlockSpec(memory_space=pltpu.VMEM)
    return pl.pallas_call(
        transform_kernel,
        out_shape=jax.ShapeDtypeStruct((6 * MODES, 128), jnp.bfloat16),
        in_specs=[vmem, vmem, pl.BlockSpec(memory_space=pl.ANY)],
        out_specs=vmem,
        scratch_shapes=[
            pltpu.VMEM((NLON, EMBED), jnp.bfloat16),
            pltpu.VMEM((2 * MODES, NLON), jnp.bfloat16),
            pltpu.VMEM((6 * MODES, 128), jnp.float32),
            pltpu.SemaphoreType.DMA,
        ],
        cost_estimate=pl.CostEstimate(
            flops=800_000_000, bytes_accessed=4_000_000, transcendentals=1024
        ),
        compiler_params=pltpu.CompilerParams(vmem_limit_bytes=VMEM_LIMIT),
    )(grid, gain, table)


def pack_rows(rows):
    return rows.reshape(512, 3, 2, 128).transpose(0, 2, 1, 3).reshape(512, 2, EMBED)


def unpack_rows(pieces):
    return pieces.reshape(512, 2, 3, 128).transpose(0, 2, 1, 3).reshape(3072, 128)


def legendre_kernel(
    coef_ref, cos_ref, start_ref, exponent_ref, weights_ref, table_ref, forward_ref, inverse_ref, held_ref
):
    held_ref[...] = table_ref[...]
    cos_rows = cos_ref[...]
    start = start_ref[...]
    weights = weights_ref[...]

    def block(index, state):
        one, two, power = state
        base = index * 16
        parts = []
        for half in range(2):
            rows = []
            for k in range(8):
                level = base + 8 * half + k
                a = coef_ref[0, level]
                b = coef_ref[1, level]
                s = coef_ref[2, level]
                one, two = (a * cos_rows) * one - b * two + s * start, one
                rows.append(one)
            scale = jnp.exp2(power)
            parts.append(
                [
                    jnp.concatenate([row[n : n + 1] for row in rows], axis=0) * scale[n : n + 1]
                    for n in range(2)
                ]
            )
            large = jnp.abs(one) > 1000.0
            factor = jnp.where(large, 2.0**-40, 1.0)
            power = power + jnp.where(large, 40.0, 0.0)
            one, two = one * factor, two * factor
        joined = [jnp.concatenate([parts[0][n], parts[1][n]], axis=0) for n in range(2)]
        here = pl.ds(pl.multiple_of(base, 16), 16)
        forward_ref[here, :] = (joined[0] * weights).astype(jnp.bfloat16)
        inverse_ref[here, :] = joined[1].astype(jnp.bfloat16)
        return one, two, power

    zeros = jnp.zeros((2, NLAT), jnp.float32)
    lax.fori_loop(0, DEGREES // 16, block, (zeros, zeros, exponent_ref[...]))


def legendre_tables(order, table):
    theta, weights = grid_points()
    theta_rows = np.stack([theta, theta[permuted_latitudes()]])
    cos_rows = jnp.asarray(np.cos(theta_rows), jnp.float32)
    log_sine = jnp.asarray(np.log2(np.sin(theta_rows)), jnp.float32)
    starts = jnp.asarray(order_starts(), jnp.float32)
    start = jnp.sum(jnp.where(jnp.arange(MODES) == order, starts, 0.0))
    m = order.astype(jnp.float32)
    log_start = start + m * log_sine
    exponent = jnp.floor(log_start)
    mantissa = jnp.exp2(log_start - exponent)
    level = jnp.arange(DEGREES, dtype=jnp.float32)
    denom = jnp.maximum(level * level - m * m, 1.0)
    above = level > m
    coef_a = jnp.where(above, jnp.sqrt(jnp.maximum(4.0 * level * level - 1.0, 1.0) / denom), 0.0)
    coef_b = jnp.sqrt(
        jnp.maximum((level - 1.0) * (level - 1.0) - m * m, 0.0)
        * (2.0 * level + 1.0)
        / (denom * jnp.maximum(2.0 * level - 3.0, 1.0))
    )
    coef_b = jnp.where(above, coef_b, 0.0)
    first = jnp.where(level == m, 1.0, 0.0)
    coefs = jnp.stack([coef_a, coef_b, first])
    vmem = pl.BlockSpec(memory_space=pltpu.VMEM)
    return pl.pallas_call(
        legendre_kernel,
        out_shape=(
            jax.ShapeDtypeStruct((DEGREES, NLAT), jnp.bfloat16),
            jax.ShapeDtypeStruct((DEGREES, NLAT), jnp.bfloat16),
            jax.ShapeDtypeStruct(table.shape, jnp.bfloat16),
        ),
        in_specs=[pl.BlockSpec(memory_space=pltpu.SMEM)] + [vmem] * 5,
        out_specs=(vmem, vmem, vmem),
        cost_estimate=pl.CostEstimate(
            flops=40_000_000, bytes_accessed=8_000_000, transcendentals=65536
        ),
        compiler_params=pltpu.CompilerParams(vmem_limit_bytes=VMEM_LIMIT),
    )(
        coefs,
        cos_rows,
        mantissa,
        exponent,
        jnp.asarray(weights, jnp.float32).reshape(1, NLAT),
        table,
    )


def mix_kernel(
    arrived_ref, forward_ref, gain_ref, weight_ref, inverse_ref, out_ref, wide_ref, field_ref
):
    wide_ref[...] = arrived_ref[...].astype(jnp.float32)
    gain = gain_ref[...]
    parts = []
    for r in range(2):
        spectrum = jnp.concatenate(
            [wide_ref[pl.ds(2 * t + r, 512, stride=6), :].astype(jnp.bfloat16) for t in range(3)],
            axis=1,
        )
        coeffs = jnp.dot(forward_ref[...], spectrum, preferred_element_type=jnp.float32)
        parts.append((coeffs * gain).astype(jnp.bfloat16))
    scaled = jnp.concatenate(parts, axis=1)
    mixed = lax.dot_general(
        weight_ref[...], scaled, (((1,), (1,)), ((), ())), preferred_element_type=jnp.float32
    ).astype(jnp.bfloat16)
    field_ref[...] = jnp.dot(mixed, inverse_ref[...], preferred_element_type=jnp.float32)
    lane = lax.broadcasted_iota(jnp.int32, (8, 128), 1)
    masks = {d: (lane & d) != 0 for d in (1, 2, 4, 8)}

    def group(index, carry):
        rows = pl.multiple_of(index // 4 * 16, 16)
        high = index % 4
        columns = pl.ds(pl.multiple_of(high * 128, 128), 128)
        halves = []
        for half in range(2):
            pieces = []
            for i in range(16):
                piece = field_ref[pl.ds(48 * i + rows + 8 * half, 8), columns]
                pieces.append(pltpu.roll(piece, i, 1) if i else piece)
            for d in (1, 2, 4, 8):
                pieces = [
                    jnp.where(masks[d], pieces[(k + d) % 16], pieces[k]) for k in range(16)
                ]
            halves.append(
                [pieces[0]] + [pltpu.roll(pieces[16 - low], 128 - low, 1) for low in range(1, 16)]
            )
        for low in range(16):
            both = jnp.concatenate([halves[0][low], halves[1][low]], axis=0)
            out_ref[high * 16 + low, pl.ds(rows, 16), :] = both.astype(jnp.bfloat16)
        return carry

    lax.fori_loop(0, 12, group, 0)


def mix_and_return(arrived, forward_table, gain, weight, inverse_table):
    vmem = pl.BlockSpec(memory_space=pltpu.VMEM)
    return pl.pallas_call(
        mix_kernel,
        out_shape=jax.ShapeDtypeStruct((64, 48, 128), jnp.bfloat16),
        in_specs=[vmem] * 5,
        out_specs=vmem,
        scratch_shapes=[
            pltpu.VMEM((6 * NLAT, 128), jnp.float32),
            pltpu.VMEM((2 * EMBED, NLAT), jnp.float32),
        ],
        cost_estimate=pl.CostEstimate(
            flops=1_400_000_000, bytes_accessed=4_000_000, transcendentals=0
        ),
        compiler_params=pltpu.CompilerParams(vmem_limit_bytes=VMEM_LIMIT),
    )(arrived, forward_table, gain, weight, inverse_table)


def restore_kernel(place_ref, spectrum_ref, table_ref, *refs):
    grid_refs, out_ref, field_ref = refs[:8], refs[8], refs[9]
    field_ref[...] = lax.dot_general(
        spectrum_ref[...],
        table_ref[...],
        (((0,), (0,)), ((), ())),
        preferred_element_type=jnp.float32,
    )
    for k in range(8):
        columns = pl.ds(pl.multiple_of(place_ref[k] * 128, 128), 128)
        for a in range(8):
            for t in range(3):
                piece = field_ref[(8 * t + a) * 16 : (8 * t + a) * 16 + 16, columns]
                rows = slice(16 * t, 16 * t + 16)
                own = grid_refs[k][a, rows, :].astype(jnp.float32)
                out_ref[a, rows, columns] = (own + piece).astype(jnp.bfloat16)


def restore(spectrum, table, grids, places):
    vmem = pl.BlockSpec(memory_space=pltpu.VMEM)
    return pl.pallas_call(
        restore_kernel,
        out_shape=jax.ShapeDtypeStruct((8, 48, NLON), jnp.bfloat16),
        in_specs=[pl.BlockSpec(memory_space=pltpu.SMEM)] + [vmem] * 10,
        out_specs=vmem,
        scratch_shapes=[pltpu.VMEM((EMBED, NLON), jnp.float32)],
        cost_estimate=pl.CostEstimate(
            flops=800_000_000, bytes_accessed=4_000_000, transcendentals=0
        ),
        compiler_params=pltpu.CompilerParams(vmem_limit_bytes=VMEM_LIMIT),
    )(places, spectrum, table, *grids)


def mix_weight(channel_mix):
    paired = pair_weight(channel_mix).T.reshape(2, 24, 16, 2 * EMBED)
    return paired.transpose(2, 1, 0, 3).reshape(2 * EMBED, 2 * EMBED)


def on_device(grid_field, norm_gain, degree_gain, channel_mix):
    both = ("lat", "chan")
    place = lax.axis_index("chan")
    forward_dft, inverse_dft = dft_tables()
    own = lax.all_to_all(grid_field, "chan", split_axis=0, concat_axis=0, tiled=True)
    own = own.reshape(NLON, EMBED)
    spectrum = pack_rows(transform(own, norm_gain.reshape(1, EMBED), jnp.asarray(forward_dft)))
    spectrum, grid_later, channel_mix = lax.optimization_barrier(
        (spectrum, grid_field, channel_mix)
    )
    arrived = lax.all_to_all(spectrum, both, split_axis=0, concat_axis=0, tiled=True)
    forward_table, inverse_table, table = legendre_tables(
        lax.axis_index(both), jnp.asarray(inverse_dft)
    )
    weight = mix_weight(channel_mix)
    pieces = grid_later.transpose(0, 2, 1).reshape(8, 8, 48, 128).transpose(1, 0, 2, 3)
    grids = [lax.dynamic_index_in_dim(pieces, place ^ k, 0, keepdims=False) for k in range(8)]
    grids = [grids[0]] + [
        lax.ppermute(grids[k], "chan", [(i, i ^ k) for i in range(8)]) for k in range(1, 8)
    ]
    places = jnp.arange(8, dtype=jnp.int32) ^ place
    arrived, forward_table, inverse_table, weight = lax.optimization_barrier(
        (arrived, forward_table, inverse_table, weight)
    )
    field = mix_and_return(unpack_rows(arrived), forward_table, degree_gain, weight, inverse_table)
    returned = lax.all_to_all(
        pack_rows(field.reshape(3072, 128)), both, split_axis=0, concat_axis=0, tiled=True
    )
    block_out = restore(returned.reshape(2 * MODES, EMBED), table, grids, places)
    return block_out.transpose(0, 2, 1)


def solution(mesh):
    return jax.shard_map(
        on_device,
        mesh=mesh,
        in_specs=(P("lat", "chan", None), P(), P(), P()),
        out_specs=P("lat", None, "chan"),
        check_vma=False,
    )
```

```python
import math

import jax
import jax.numpy as jnp
import numpy as np
from jax import lax
from jax.experimental import pallas as pl
from jax.experimental.pallas import tpu as pltpu
from jax.sharding import PartitionSpec as P

NLAT = 512
EMBED = 384
NLON = 1024
DEGREES = 512
MODES = 512
VMEM_LIMIT = 20 * 1024 * 1024


def grid_points():
    theta = math.pi * (np.arange(NLAT, dtype=np.float64) + 0.5) / NLAT
    harmonic = np.arange(1, NLAT // 2 + 1, dtype=np.float64)
    series = np.sum(
        np.cos(2.0 * harmonic[None, :] * theta[:, None]) / (4.0 * harmonic * harmonic - 1.0),
        axis=1,
    )
    weights = 2.0 / NLAT * (1.0 - 2.0 * series)
    return theta, weights


def order_starts():
    return np.array(
        [
            0.5 * (math.lgamma(m + 1.5) - math.lgamma(1.5) - math.lgamma(m + 1.0) - math.log(2.0))
            / math.log(2.0)
            for m in range(MODES)
        ]
    )


def dft_tables():
    phase = np.arange(MODES)[:, None] * np.arange(NLON)[None, :] % NLON
    angle = 2.0 * math.pi / NLON * phase
    parts = np.stack([np.cos(angle), -np.sin(angle)], axis=1)
    factor = np.where(np.arange(MODES) == 0, 1.0, 2.0)[:, None, None]
    forward = (parts / NLON).reshape(2, MODES // 2, 2, NLON).transpose(0, 2, 1, 3)
    forward = forward.reshape(2 * MODES, NLON)
    inverse = (parts * factor).transpose(1, 0, 2).reshape(2 * MODES, NLON)
    return forward.astype(jnp.bfloat16), inverse.astype(jnp.bfloat16)


def pair_weight(channel_mix):
    real_part = channel_mix[0]
    imag_part = channel_mix[1]
    upper = jnp.concatenate([real_part, imag_part], axis=1)
    lower = jnp.concatenate([-imag_part, real_part], axis=1)
    return jnp.concatenate([upper, lower], axis=0)


def permuted_latitudes():
    high, a, low = np.meshgrid(np.arange(4), np.arange(8), np.arange(16), indexing="ij")
    return ((16 * high + low) * 8 + a).reshape(-1)


def hold_kernel(table_ref, out_ref):
    out_ref[...] = table_ref[...]


def hold(table):
    vmem = pl.BlockSpec(memory_space=pltpu.VMEM)
    return pl.pallas_call(
        hold_kernel,
        out_shape=jax.ShapeDtypeStruct(table.shape, table.dtype),
        in_specs=[vmem],
        out_specs=vmem,
        cost_estimate=pl.CostEstimate(flops=0, bytes_accessed=4_000_000, transcendentals=0),
        compiler_params=pltpu.CompilerParams(vmem_limit_bytes=VMEM_LIMIT),
    )(table)


def transform_kernel(
    weights_ref, grid_ref, gain_ref, table_ref, out_ref, normed_ref, wide_ref, narrow_ref, out_sems
):
    row = lax.axis_index("lat") * 8 + lax.axis_index("chan")
    spot = lax.broadcasted_iota(jnp.int32, (4, 128), 0) * 128
    spot = spot + lax.broadcasted_iota(jnp.int32, (4, 128), 1)
    share = jnp.sum(jnp.where(spot == row, weights_ref[...], 0.0), axis=1, keepdims=True)
    share = jnp.sum(share, axis=0, keepdims=True)
    gain = gain_ref[...]
    for piece in range(8):
        rows = slice(128 * piece, 128 * piece + 128)
        values = grid_ref[rows, :].astype(jnp.float32)
        mean_value = jnp.mean(values, axis=1, keepdims=True)
        centered = values - mean_value
        variance = jnp.mean(centered * centered, axis=1, keepdims=True)
        normed_ref[rows, :] = (centered * lax.rsqrt(variance + 1e-05) * gain).astype(jnp.bfloat16)
    results = []
    for half in range(2):
        spectrum = jnp.dot(
            table_ref[512 * half : 512 * half + 512, :],
            normed_ref[...],
            preferred_element_type=jnp.float32,
        )
        spectrum = spectrum * share
        first = 1536 * half
        for r in range(2):
            for t in range(3):
                wide_ref[pl.ds(first + 2 * t + r, 256, stride=6), :] = spectrum[
                    256 * r : 256 * r + 256, 128 * t : 128 * t + 128
                ]
        rows = slice(first, first + 1536)
        narrow_ref[rows, :] = wide_ref[rows, :].astype(jnp.bfloat16)
        results.append(
            pltpu.make_async_copy(narrow_ref.at[rows], out_ref.at[rows], out_sems.at[half])
        )
        results[half].start()
    for half in range(2):
        results[half].wait()


def transform(weights, grid, gain, table):
    vmem = pl.BlockSpec(memory_space=pltpu.VMEM)
    return pl.pallas_call(
        transform_kernel,
        out_shape=jax.ShapeDtypeStruct((6 * MODES, 128), jnp.bfloat16),
        in_specs=[vmem] * 4,
        out_specs=pl.BlockSpec(memory_space=pltpu.MemorySpace.HBM),
        scratch_shapes=[
            pltpu.VMEM((NLON, EMBED), jnp.bfloat16),
            pltpu.VMEM((6 * MODES, 128), jnp.float32),
            pltpu.VMEM((6 * MODES, 128), jnp.bfloat16),
            pltpu.SemaphoreType.DMA((2,)),
        ],
        cost_estimate=pl.CostEstimate(
            flops=800_000_000, bytes_accessed=4_000_000, transcendentals=1024
        ),
        compiler_params=pltpu.CompilerParams(vmem_limit_bytes=VMEM_LIMIT),
    )(weights, grid, gain, table)


def spread_rows(source_ref, wide_ref, pieces_ref):
    wide_ref[...] = source_ref[...].astype(jnp.float32)
    for r in range(2):
        for t in range(3):
            pieces_ref[512 * r : 512 * r + 512, 128 * t : 128 * t + 128] = wide_ref[
                pl.ds(2 * t + r, 512, stride=6), :
            ].astype(jnp.bfloat16)


def pack_rows(rows):
    return rows.reshape(512, 3, 2, 128).transpose(0, 2, 1, 3).reshape(512, 2, EMBED)


def unpack_rows(pieces):
    return pieces.reshape(512, 2, 3, 128).transpose(0, 2, 1, 3).reshape(3072, 128)


def legendre_kernel(coef_ref, cos_ref, start_ref, exponent_ref, table_ref):
    cos_row = cos_ref[...]
    start = start_ref[...]

    def block(index, state):
        one, two, power = state
        base = index * 16
        parts = []
        for half in range(2):
            rows = []
            for k in range(8):
                level = base + 8 * half + k
                a = coef_ref[0, level]
                b = coef_ref[1, level]
                s = coef_ref[2, level]
                one, two = (a * cos_row) * one - b * two + s * start, one
                rows.append(one)
            parts.append(jnp.concatenate(rows, axis=0) * jnp.exp2(power))
            large = jnp.abs(one) > 1000.0
            factor = jnp.where(large, 2.0**-40, 1.0)
            power = power + jnp.where(large, 40.0, 0.0)
            one, two = one * factor, two * factor
        here = pl.ds(pl.multiple_of(base, 16), 16)
        table_ref[here, :] = jnp.concatenate(parts, axis=0).astype(jnp.bfloat16)
        return one, two, power

    zeros = jnp.zeros((1, NLAT), jnp.float32)
    lax.fori_loop(0, DEGREES // 16, block, (zeros, zeros, exponent_ref[...]))


def legendre_table(order):
    theta_row = grid_points()[0][permuted_latitudes()].reshape(1, NLAT)
    cos_row = jnp.asarray(np.cos(theta_row), jnp.float32)
    log_sine = jnp.asarray(np.log2(np.sin(theta_row)), jnp.float32)
    starts = jnp.asarray(order_starts(), jnp.float32)
    start = jnp.sum(jnp.where(jnp.arange(MODES) == order, starts, 0.0))
    m = order.astype(jnp.float32)
    log_start = start + m * log_sine
    exponent = jnp.floor(log_start)
    mantissa = jnp.exp2(log_start - exponent)
    level = jnp.arange(DEGREES, dtype=jnp.float32)
    denom = jnp.maximum(level * level - m * m, 1.0)
    above = level > m
    coef_a = jnp.where(above, jnp.sqrt(jnp.maximum(4.0 * level * level - 1.0, 1.0) / denom), 0.0)
    coef_b = jnp.sqrt(
        jnp.maximum((level - 1.0) * (level - 1.0) - m * m, 0.0)
        * (2.0 * level + 1.0)
        / (denom * jnp.maximum(2.0 * level - 3.0, 1.0))
    )
    coef_b = jnp.where(above, coef_b, 0.0)
    first = jnp.where(level == m, 1.0, 0.0)
    coefs = jnp.stack([coef_a, coef_b, first])
    vmem = pl.BlockSpec(memory_space=pltpu.VMEM)
    return pl.pallas_call(
        legendre_kernel,
        out_shape=jax.ShapeDtypeStruct((DEGREES, NLAT), jnp.bfloat16),
        in_specs=[pl.BlockSpec(memory_space=pltpu.SMEM)] + [vmem] * 3,
        out_specs=vmem,
        cost_estimate=pl.CostEstimate(
            flops=40_000_000, bytes_accessed=8_000_000, transcendentals=65536
        ),
        compiler_params=pltpu.CompilerParams(vmem_limit_bytes=VMEM_LIMIT),
    )(coefs, cos_row, mantissa, exponent)


def mix_kernel(
    arrived_ref,
    table_ref,
    gain_ref,
    weight_ref,
    spare_ref,
    out_ref,
    wide_ref,
    pieces_ref,
    field_ref,
    narrow_ref,
    out_sems,
):
    wide_ref[...] = arrived_ref[...].astype(jnp.float32)
    for r in range(2):
        for high in range(4):
            for a in range(8):
                rows = slice(512 * r + 128 * high + 16 * a, 512 * r + 128 * high + 16 * a + 16)
                for t in range(3):
                    first = 768 * high + 6 * a + 2 * t + r
                    pieces_ref[rows, 128 * t : 128 * t + 128] = wide_ref[
                        pl.ds(first, 16, stride=48), :
                    ].astype(jnp.bfloat16)
    gain = gain_ref[...]
    parts = []
    for r in range(2):
        coeffs = jnp.dot(
            table_ref[...],
            pieces_ref[512 * r : 512 * r + 512, :],
            preferred_element_type=jnp.float32,
        )
        parts.append((coeffs * gain).astype(jnp.bfloat16))
    scaled = jnp.concatenate(parts, axis=1)
    mixed = lax.dot_general(
        weight_ref[...], scaled, (((1,), (1,)), ((), ())), preferred_element_type=jnp.float32
    ).astype(jnp.bfloat16)
    lane = lax.broadcasted_iota(jnp.int32, (8, 128), 1)
    masks = {d: (lane & d) != 0 for d in (1, 2, 4, 8)}
    results = []
    for pair in range(2):
        field_ref[:, 256 * pair : 256 * pair + 256] = jnp.dot(
            mixed, table_ref[:, 256 * pair : 256 * pair + 256], preferred_element_type=jnp.float32
        )
    for high in range(4):
        columns = slice(128 * high, 128 * high + 128)

        def group(index, carry, high=high, columns=columns):
            rows = pl.multiple_of(index * 16, 16)
            halves = []
            for half in range(2):
                pieces = []
                for i in range(16):
                    piece = field_ref[pl.ds(48 * i + rows + 8 * half, 8), columns]
                    pieces.append(pltpu.roll(piece, i, 1) if i else piece)
                for d in (1, 2, 4, 8):
                    pieces = [
                        jnp.where(masks[d], pieces[(k + d) % 16], pieces[k]) for k in range(16)
                    ]
                halves.append([pieces[(16 - low) % 16] for low in range(16)])
            for low in range(16):
                both = jnp.concatenate([halves[0][low], halves[1][low]], axis=0)
                here = pl.ds(48 * (high * 16 + low) + rows, 16)
                narrow_ref[here, :] = both.astype(jnp.bfloat16)
            return carry

        lax.fori_loop(0, 3, group, 0)
        here = slice(768 * high, 768 * high + 768)
        results.append(
            pltpu.make_async_copy(narrow_ref.at[here], out_ref.at[here], out_sems.at[high])
        )
        results[high].start()
    for high in range(4):
        results[high].wait()


def mix_and_return(arrived, table, gain, weight, spare):
    vmem = pl.BlockSpec(memory_space=pltpu.VMEM)
    return pl.pallas_call(
        mix_kernel,
        out_shape=jax.ShapeDtypeStruct((6 * MODES, 128), jnp.bfloat16),
        in_specs=[vmem] * 4 + [pl.BlockSpec(memory_space=pltpu.MemorySpace.HBM)],
        out_specs=pl.BlockSpec(memory_space=pltpu.MemorySpace.HBM),
        input_output_aliases={4: 0},
        scratch_shapes=[
            pltpu.VMEM((6 * NLAT, 128), jnp.float32),
            pltpu.VMEM((2 * NLAT, EMBED), jnp.bfloat16),
            pltpu.VMEM((2 * EMBED, NLAT), jnp.float32),
            pltpu.VMEM((6 * MODES, 128), jnp.bfloat16),
            pltpu.SemaphoreType.DMA((4,)),
        ],
        cost_estimate=pl.CostEstimate(
            flops=1_400_000_000, bytes_accessed=4_000_000, transcendentals=0
        ),
        compiler_params=pltpu.CompilerParams(vmem_limit_bytes=VMEM_LIMIT),
    )(arrived, table, gain, weight, spare)


def gather_kernel(place_ref, table_ref, *refs):
    grid_refs, out_ref = refs[:8], refs[8]
    for k in range(8):
        columns = pl.ds(pl.multiple_of(place_ref[k] * 128, 128), 128)
        out_ref[:, :, columns] = grid_refs[k][...]


def gather(places, table, grids):
    vmem = pl.BlockSpec(memory_space=pltpu.VMEM)
    return pl.pallas_call(
        gather_kernel,
        out_shape=jax.ShapeDtypeStruct((8, 48, NLON), jnp.bfloat16),
        in_specs=[pl.BlockSpec(memory_space=pltpu.SMEM)] + [vmem] * 9,
        out_specs=vmem,
        cost_estimate=pl.CostEstimate(flops=0, bytes_accessed=6_000_000, transcendentals=0),
        compiler_params=pltpu.CompilerParams(vmem_limit_bytes=VMEM_LIMIT),
    )(places, table, *grids)


def restore_kernel(
    spectrum_ref,
    table_ref,
    grid_ref,
    out_ref,
    wide_ref,
    pieces_ref,
    field_ref,
    held_ref,
    narrow_ref,
    grid_sem,
    out_sems,
):
    grid_copy = pltpu.make_async_copy(grid_ref, held_ref, grid_sem)
    grid_copy.start()
    spread_rows(spectrum_ref, wide_ref, pieces_ref)
    field = lax.dot_general(
        pieces_ref[...],
        table_ref[...],
        (((0,), (0,)), ((), ())),
        preferred_element_type=jnp.float32,
    )
    for t in range(3):
        for s in range(8):
            columns = slice(128 * s, 128 * s + 128)
            field_ref[pl.ds(1152 * t + s, 128, stride=8), :] = field[128 * t : 128 * t + 128, columns]
            field_ref[pl.ds(1152 * t + 1024 + s, 16, stride=8), :] = field[
                128 * t : 128 * t + 16, columns
            ]
    turn = pl.multiple_of(lax.rem(lax.axis_index("lat"), 16) * 8, 8)
    grid_copy.wait()
    results = []
    for a in range(8):
        for t in range(3):
            first = 8 * (144 * t + 16 * a)
            piece = jnp.concatenate(
                [field_ref[pl.ds(first + turn + s, 16, stride=8), :] for s in range(8)], axis=1
            )
            rows = slice(16 * t, 16 * t + 16)
            own = held_ref[a, rows, :].astype(jnp.float32)
            narrow_ref[a, rows, :] = (own + piece).astype(jnp.bfloat16)
        results.append(pltpu.make_async_copy(narrow_ref.at[a], out_ref.at[a], out_sems.at[a]))
        results[a].start()
    for a in range(8):
        results[a].wait()


def restore(spectrum, table, grid):
    vmem = pl.BlockSpec(memory_space=pltpu.VMEM)
    return pl.pallas_call(
        restore_kernel,
        out_shape=jax.ShapeDtypeStruct((8, 48, NLON), jnp.bfloat16),
        in_specs=[vmem, vmem, pl.BlockSpec(memory_space=pltpu.MemorySpace.HBM)],
        out_specs=pl.BlockSpec(memory_space=pltpu.MemorySpace.HBM),
        input_output_aliases={2: 0},
        scratch_shapes=[
            pltpu.VMEM((6 * MODES, 128), jnp.float32),
            pltpu.VMEM((2 * MODES, EMBED), jnp.bfloat16),
            pltpu.VMEM((3 * 144 * 8, 128), jnp.float32),
            pltpu.VMEM((8, 48, NLON), jnp.bfloat16),
            pltpu.VMEM((8, 48, NLON), jnp.bfloat16),
            pltpu.SemaphoreType.DMA,
            pltpu.SemaphoreType.DMA((8,)),
        ],
        cost_estimate=pl.CostEstimate(
            flops=800_000_000, bytes_accessed=4_000_000, transcendentals=0
        ),
        compiler_params=pltpu.CompilerParams(vmem_limit_bytes=VMEM_LIMIT),
    )(spectrum, table, grid)


def mix_weight(channel_mix):
    paired = pair_weight(channel_mix).T.reshape(2, 24, 16, 2 * EMBED)
    return paired.transpose(2, 1, 0, 3).reshape(2 * EMBED, 2 * EMBED)


def on_device(grid_field, norm_gain, degree_gain, channel_mix):
    both = ("lat", "chan")
    place = lax.axis_index("chan")
    forward_dft, inverse_dft = dft_tables()
    own = lax.all_to_all(grid_field, "chan", split_axis=0, concat_axis=0, tiled=True)
    own = own.reshape(NLON, EMBED)
    weights = jnp.asarray(grid_points()[1].reshape(4, 128), jnp.float32)
    own, forward_dft = lax.optimization_barrier((own, hold(jnp.asarray(forward_dft))))
    rows = transform(weights, own, norm_gain.reshape(1, EMBED), forward_dft)
    spectrum = pack_rows(rows)
    spectrum, grid_later, channel_mix = lax.optimization_barrier(
        (spectrum, grid_field, channel_mix)
    )
    arrived = lax.all_to_all(spectrum, both, split_axis=0, concat_axis=0, tiled=True)
    legendre = legendre_table(lax.axis_index(both))
    weight = mix_weight(channel_mix)
    pieces = grid_later.transpose(0, 2, 1).reshape(8, 8, 48, 128).transpose(1, 0, 2, 3)
    grids = [lax.dynamic_index_in_dim(pieces, place ^ k, 0, keepdims=False) for k in range(8)]
    grids = [grids[0]] + [
        lax.ppermute(grids[k], "chan", [(i, i ^ k) for i in range(8)]) for k in range(1, 8)
    ]
    places = jnp.arange(8, dtype=jnp.int32) ^ place
    field = mix_and_return(unpack_rows(arrived), legendre, degree_gain, weight, rows)
    returned = lax.all_to_all(
        pack_rows(field), both, split_axis=0, concat_axis=0, tiled=True
    )
    table = jnp.asarray(inverse_dft)
    grid = gather(places, table, grids)
    block_out = restore(unpack_rows(returned), table, grid)
    return block_out.transpose(0, 2, 1)


def solution(mesh):
    return jax.shard_map(
        on_device,
        mesh=mesh,
        in_specs=(P("lat", "chan", None), P(), P(), P()),
        out_specs=P("lat", None, "chan"),
        check_vma=False,
    )
```

```python
import math

import jax
import jax.numpy as jnp
import numpy as np
from jax import lax
from jax.experimental import pallas as pl
from jax.experimental.pallas import tpu as pltpu
from jax.sharding import PartitionSpec as P

NLAT = 512
EMBED = 384
NLON = 1024
DEGREES = 512
MODES = 512
VMEM_LIMIT = 20 * 1024 * 1024


def grid_points():
    theta = math.pi * (np.arange(NLAT, dtype=np.float64) + 0.5) / NLAT
    harmonic = np.arange(1, NLAT // 2 + 1, dtype=np.float64)
    series = np.sum(
        np.cos(2.0 * harmonic[None, :] * theta[:, None]) / (4.0 * harmonic * harmonic - 1.0),
        axis=1,
    )
    weights = 2.0 / NLAT * (1.0 - 2.0 * series)
    return theta, weights


def order_starts():
    return np.array(
        [
            0.5 * (math.lgamma(m + 1.5) - math.lgamma(1.5) - math.lgamma(m + 1.0) - math.log(2.0))
            / math.log(2.0)
            for m in range(MODES)
        ]
    )


def dft_tables():
    phase = np.arange(MODES)[:, None] * np.arange(NLON)[None, :] % NLON
    angle = 2.0 * math.pi / NLON * phase
    parts = np.stack([np.cos(angle), -np.sin(angle)], axis=1)
    factor = np.where(np.arange(MODES) == 0, 1.0, 2.0)[:, None, None]
    forward = (parts / NLON).reshape(2, MODES // 2, 2, NLON).transpose(0, 2, 1, 3)
    forward = forward.reshape(2 * MODES, NLON)
    inverse = (parts * factor).transpose(1, 0, 2).reshape(2 * MODES, NLON)
    return forward.astype(jnp.bfloat16), inverse.astype(jnp.bfloat16)


def pair_weight(channel_mix):
    real_part = channel_mix[0]
    imag_part = channel_mix[1]
    upper = jnp.concatenate([real_part, imag_part], axis=1)
    lower = jnp.concatenate([-imag_part, real_part], axis=1)
    return jnp.concatenate([upper, lower], axis=0)


def permuted_latitudes():
    high, a, low = np.meshgrid(np.arange(4), np.arange(8), np.arange(16), indexing="ij")
    return ((16 * high + low) * 8 + a).reshape(-1)


def hold_kernel(table_ref, out_ref):
    out_ref[...] = table_ref[...]


def hold(table):
    vmem = pl.BlockSpec(memory_space=pltpu.VMEM)
    return pl.pallas_call(
        hold_kernel,
        out_shape=jax.ShapeDtypeStruct(table.shape, table.dtype),
        in_specs=[vmem],
        out_specs=vmem,
        cost_estimate=pl.CostEstimate(flops=0, bytes_accessed=4_000_000, transcendentals=0),
        compiler_params=pltpu.CompilerParams(vmem_limit_bytes=VMEM_LIMIT),
    )(table)


def transform_kernel(
    weights_ref, grid_ref, gain_ref, table_ref, out_ref, normed_ref, wide_ref, narrow_ref, out_sems
):
    row = lax.axis_index("lat") * 8 + lax.axis_index("chan")
    spot = lax.broadcasted_iota(jnp.int32, (4, 128), 0) * 128
    spot = spot + lax.broadcasted_iota(jnp.int32, (4, 128), 1)
    share = jnp.sum(jnp.where(spot == row, weights_ref[...], 0.0), axis=1, keepdims=True)
    share = jnp.sum(share, axis=0, keepdims=True)
    gain = gain_ref[...]
    for piece in range(8):
        rows = slice(128 * piece, 128 * piece + 128)
        values = grid_ref[rows, :].astype(jnp.float32)
        mean_value = jnp.mean(values, axis=1, keepdims=True)
        centered = values - mean_value
        variance = jnp.mean(centered * centered, axis=1, keepdims=True)
        normed_ref[rows, :] = (centered * lax.rsqrt(variance + 1e-05) * gain).astype(jnp.bfloat16)
    results = []
    for half in range(2):
        spectrum = jnp.dot(
            table_ref[512 * half : 512 * half + 512, :],
            normed_ref[...],
            preferred_element_type=jnp.float32,
        )
        spectrum = spectrum * share
        first = 1536 * half
        for r in range(2):
            for t in range(3):
                wide_ref[pl.ds(first + 2 * t + r, 256, stride=6), :] = spectrum[
                    256 * r : 256 * r + 256, 128 * t : 128 * t + 128
                ]
        rows = slice(first, first + 1536)
        narrow_ref[rows, :] = wide_ref[rows, :].astype(jnp.bfloat16)
        results.append(
            pltpu.make_async_copy(narrow_ref.at[rows], out_ref.at[rows], out_sems.at[half])
        )
        results[half].start()
    for half in range(2):
        results[half].wait()


def transform(weights, grid, gain, table):
    vmem = pl.BlockSpec(memory_space=pltpu.VMEM)
    return pl.pallas_call(
        transform_kernel,
        out_shape=jax.ShapeDtypeStruct((6 * MODES, 128), jnp.bfloat16),
        in_specs=[vmem] * 4,
        out_specs=pl.BlockSpec(memory_space=pltpu.MemorySpace.HBM),
        scratch_shapes=[
            pltpu.VMEM((NLON, EMBED), jnp.bfloat16),
            pltpu.VMEM((6 * MODES, 128), jnp.float32),
            pltpu.VMEM((6 * MODES, 128), jnp.bfloat16),
            pltpu.SemaphoreType.DMA((2,)),
        ],
        cost_estimate=pl.CostEstimate(
            flops=800_000_000, bytes_accessed=4_000_000, transcendentals=1024
        ),
        compiler_params=pltpu.CompilerParams(vmem_limit_bytes=VMEM_LIMIT),
    )(weights, grid, gain, table)


def spread_rows(source_ref, wide_ref, pieces_ref):
    wide_ref[...] = source_ref[...].astype(jnp.float32)
    for r in range(2):
        for t in range(3):
            pieces_ref[512 * r : 512 * r + 512, 128 * t : 128 * t + 128] = wide_ref[
                pl.ds(2 * t + r, 512, stride=6), :
            ].astype(jnp.bfloat16)


def pack_rows(rows):
    return rows.reshape(512, 3, 2, 128).transpose(0, 2, 1, 3).reshape(512, 2, EMBED)


def unpack_rows(pieces):
    return pieces.reshape(512, 2, 3, 128).transpose(0, 2, 1, 3).reshape(3072, 128)


def legendre_kernel(coef_ref, cos_ref, start_ref, exponent_ref, table_ref):
    cos_row = cos_ref[...]
    start = start_ref[...]

    def block(index, state):
        one, two, power = state
        base = index * 16
        parts = []
        for half in range(2):
            rows = []
            for k in range(8):
                level = base + 8 * half + k
                a = coef_ref[0, level]
                b = coef_ref[1, level]
                s = coef_ref[2, level]
                one, two = (a * cos_row) * one - b * two + s * start, one
                rows.append(one)
            parts.append(jnp.concatenate(rows, axis=0) * jnp.exp2(power))
            large = jnp.abs(one) > 1000.0
            factor = jnp.where(large, 2.0**-40, 1.0)
            power = power + jnp.where(large, 40.0, 0.0)
            one, two = one * factor, two * factor
        here = pl.ds(pl.multiple_of(base, 16), 16)
        table_ref[here, :] = jnp.concatenate(parts, axis=0).astype(jnp.bfloat16)
        return one, two, power

    zeros = jnp.zeros((1, NLAT), jnp.float32)
    lax.fori_loop(0, DEGREES // 16, block, (zeros, zeros, exponent_ref[...]))


def legendre_table(order):
    theta_row = grid_points()[0][permuted_latitudes()].reshape(1, NLAT)
    cos_row = jnp.asarray(np.cos(theta_row), jnp.float32)
    log_sine = jnp.asarray(np.log2(np.sin(theta_row)), jnp.float32)
    starts = jnp.asarray(order_starts(), jnp.float32)
    start = jnp.sum(jnp.where(jnp.arange(MODES) == order, starts, 0.0))
    m = order.astype(jnp.float32)
    log_start = start + m * log_sine
    exponent = jnp.floor(log_start)
    mantissa = jnp.exp2(log_start - exponent)
    level = jnp.arange(DEGREES, dtype=jnp.float32)
    denom = jnp.maximum(level * level - m * m, 1.0)
    above = level > m
    coef_a = jnp.where(above, jnp.sqrt(jnp.maximum(4.0 * level * level - 1.0, 1.0) / denom), 0.0)
    coef_b = jnp.sqrt(
        jnp.maximum((level - 1.0) * (level - 1.0) - m * m, 0.0)
        * (2.0 * level + 1.0)
        / (denom * jnp.maximum(2.0 * level - 3.0, 1.0))
    )
    coef_b = jnp.where(above, coef_b, 0.0)
    first = jnp.where(level == m, 1.0, 0.0)
    coefs = jnp.stack([coef_a, coef_b, first])
    vmem = pl.BlockSpec(memory_space=pltpu.VMEM)
    return pl.pallas_call(
        legendre_kernel,
        out_shape=jax.ShapeDtypeStruct((DEGREES, NLAT), jnp.bfloat16),
        in_specs=[pl.BlockSpec(memory_space=pltpu.SMEM)] + [vmem] * 3,
        out_specs=vmem,
        cost_estimate=pl.CostEstimate(
            flops=40_000_000, bytes_accessed=8_000_000, transcendentals=65536
        ),
        compiler_params=pltpu.CompilerParams(vmem_limit_bytes=VMEM_LIMIT),
    )(coefs, cos_row, mantissa, exponent)


def mix_kernel(
    arrived_ref,
    table_ref,
    gain_ref,
    weight_ref,
    spare_ref,
    out_ref,
    wide_ref,
    pieces_ref,
    field_ref,
    narrow_ref,
    out_sems,
):
    wide_ref[...] = arrived_ref[...].astype(jnp.float32)
    for r in range(2):
        for high in range(4):
            for a in range(8):
                rows = slice(128 * high + 16 * a, 128 * high + 16 * a + 16)
                for t in range(3):
                    first = 768 * high + 6 * a + 2 * t + r
                    columns = slice(384 * r + 128 * t, 384 * r + 128 * t + 128)
                    pieces_ref[rows, columns] = wide_ref[
                        pl.ds(first, 16, stride=48), :
                    ].astype(jnp.bfloat16)
    gain = gain_ref[...]
    coeffs = jnp.dot(table_ref[...], pieces_ref[...], preferred_element_type=jnp.float32)
    scaled = (coeffs * jnp.concatenate([gain, gain], axis=1)).astype(jnp.bfloat16)
    mixed = lax.dot_general(
        weight_ref[...], scaled, (((1,), (1,)), ((), ())), preferred_element_type=jnp.float32
    ).astype(jnp.bfloat16)
    lane = lax.broadcasted_iota(jnp.int32, (8, 128), 1)
    masks = {d: (lane & d) != 0 for d in (1, 2, 4, 8)}
    results = []
    for pair in range(2):
        field_ref[:, 256 * pair : 256 * pair + 256] = jnp.dot(
            mixed, table_ref[:, 256 * pair : 256 * pair + 256], preferred_element_type=jnp.float32
        )
    for high in range(4):
        columns = slice(128 * high, 128 * high + 128)

        def group(index, carry, high=high, columns=columns):
            rows = index * 16
            halves = []
            for half in range(2):
                pieces = []
                for i in range(16):
                    piece = field_ref[pl.ds(48 * i + rows + 8 * half, 8), columns]
                    pieces.append(pltpu.roll(piece, i, 1) if i else piece)
                for d in (1, 2, 4, 8):
                    pieces = [
                        jnp.where(masks[d], pieces[(k + d) % 16], pieces[k]) for k in range(16)
                    ]
                halves.append([pieces[(16 - low) % 16] for low in range(16)])
            for low in range(16):
                both = jnp.concatenate([halves[0][low], halves[1][low]], axis=0)
                here = pl.ds(48 * (high * 16 + low) + rows, 16)
                narrow_ref[here, :] = both.astype(jnp.bfloat16)
            return carry

        for index in range(3):
            group(index, 0)
        here = slice(768 * high, 768 * high + 768)
        results.append(
            pltpu.make_async_copy(narrow_ref.at[here], out_ref.at[here], out_sems.at[high])
        )
        results[high].start()
    for high in range(4):
        results[high].wait()


def mix_and_return(arrived, table, gain, weight, spare):
    vmem = pl.BlockSpec(memory_space=pltpu.VMEM)
    return pl.pallas_call(
        mix_kernel,
        out_shape=jax.ShapeDtypeStruct((6 * MODES, 128), jnp.bfloat16),
        in_specs=[vmem] * 4 + [pl.BlockSpec(memory_space=pltpu.MemorySpace.HBM)],
        out_specs=pl.BlockSpec(memory_space=pltpu.MemorySpace.HBM),
        input_output_aliases={4: 0},
        scratch_shapes=[
            pltpu.VMEM((6 * NLAT, 128), jnp.float32),
            pltpu.VMEM((NLAT, 2 * EMBED), jnp.bfloat16),
            pltpu.VMEM((2 * EMBED, NLAT), jnp.float32),
            pltpu.VMEM((6 * MODES, 128), jnp.bfloat16),
            pltpu.SemaphoreType.DMA((4,)),
        ],
        cost_estimate=pl.CostEstimate(
            flops=1_400_000_000, bytes_accessed=4_000_000, transcendentals=0
        ),
        compiler_params=pltpu.CompilerParams(vmem_limit_bytes=VMEM_LIMIT),
    )(arrived, table, gain, weight, spare)


def gather_kernel(place_ref, table_ref, *refs):
    grid_refs, out_ref = refs[:8], refs[8]
    for k in range(8):
        columns = pl.ds(pl.multiple_of(place_ref[k] * 128, 128), 128)
        out_ref[:, :, columns] = grid_refs[k][...]


def gather(places, table, grids):
    vmem = pl.BlockSpec(memory_space=pltpu.VMEM)
    return pl.pallas_call(
        gather_kernel,
        out_shape=jax.ShapeDtypeStruct((8, 48, NLON), jnp.bfloat16),
        in_specs=[pl.BlockSpec(memory_space=pltpu.SMEM)] + [vmem] * 9,
        out_specs=vmem,
        cost_estimate=pl.CostEstimate(flops=0, bytes_accessed=6_000_000, transcendentals=0),
        compiler_params=pltpu.CompilerParams(vmem_limit_bytes=VMEM_LIMIT),
    )(places, table, *grids)


def restore_kernel(
    spectrum_ref,
    table_ref,
    grid_ref,
    out_ref,
    wide_ref,
    pieces_ref,
    field_ref,
    held_ref,
    narrow_ref,
    grid_sem,
    out_sems,
):
    grid_copy = pltpu.make_async_copy(grid_ref, held_ref, grid_sem)
    grid_copy.start()
    spread_rows(spectrum_ref, wide_ref, pieces_ref)
    field = lax.dot_general(
        pieces_ref[...],
        table_ref[...],
        (((0,), (0,)), ((), ())),
        preferred_element_type=jnp.float32,
    )
    for t in range(3):
        for s in range(8):
            columns = slice(128 * s, 128 * s + 128)
            field_ref[pl.ds(1152 * t + s, 128, stride=8), :] = field[128 * t : 128 * t + 128, columns]
            field_ref[pl.ds(1152 * t + 1024 + s, 16, stride=8), :] = field[
                128 * t : 128 * t + 16, columns
            ]
    turn = pl.multiple_of(lax.rem(lax.axis_index("lat"), 16) * 8, 8)
    grid_copy.wait()
    results = []
    for a in range(8):
        for t in range(3):
            first = 8 * (144 * t + 16 * a)
            piece = jnp.concatenate(
                [field_ref[pl.ds(first + turn + s, 16, stride=8), :] for s in range(8)], axis=1
            )
            rows = slice(16 * t, 16 * t + 16)
            own = held_ref[a, rows, :].astype(jnp.float32)
            narrow_ref[a, rows, :] = (own + piece).astype(jnp.bfloat16)
        results.append(pltpu.make_async_copy(narrow_ref.at[a], out_ref.at[a], out_sems.at[a]))
        results[a].start()
    for a in range(8):
        results[a].wait()


def restore(spectrum, table, grid):
    vmem = pl.BlockSpec(memory_space=pltpu.VMEM)
    return pl.pallas_call(
        restore_kernel,
        out_shape=jax.ShapeDtypeStruct((8, 48, NLON), jnp.bfloat16),
        in_specs=[vmem, vmem, pl.BlockSpec(memory_space=pltpu.MemorySpace.HBM)],
        out_specs=pl.BlockSpec(memory_space=pltpu.MemorySpace.HBM),
        input_output_aliases={2: 0},
        scratch_shapes=[
            pltpu.VMEM((6 * MODES, 128), jnp.float32),
            pltpu.VMEM((2 * MODES, EMBED), jnp.bfloat16),
            pltpu.VMEM((3 * 144 * 8, 128), jnp.float32),
            pltpu.VMEM((8, 48, NLON), jnp.bfloat16),
            pltpu.VMEM((8, 48, NLON), jnp.bfloat16),
            pltpu.SemaphoreType.DMA,
            pltpu.SemaphoreType.DMA((8,)),
        ],
        cost_estimate=pl.CostEstimate(
            flops=800_000_000, bytes_accessed=4_000_000, transcendentals=0
        ),
        compiler_params=pltpu.CompilerParams(vmem_limit_bytes=VMEM_LIMIT),
    )(spectrum, table, grid)


def mix_weight(channel_mix):
    paired = pair_weight(channel_mix).T.reshape(2, 24, 16, 2 * EMBED)
    return paired.transpose(2, 1, 0, 3).reshape(2 * EMBED, 2 * EMBED)


def on_device(grid_field, norm_gain, degree_gain, channel_mix):
    both = ("lat", "chan")
    place = lax.axis_index("chan")
    forward_dft, inverse_dft = dft_tables()
    own = lax.all_to_all(grid_field, "chan", split_axis=0, concat_axis=0, tiled=True)
    own = own.reshape(NLON, EMBED)
    weights = jnp.asarray(grid_points()[1].reshape(4, 128), jnp.float32)
    own, forward_dft = lax.optimization_barrier((own, hold(jnp.asarray(forward_dft))))
    rows = transform(weights, own, norm_gain.reshape(1, EMBED), forward_dft)
    spectrum = pack_rows(rows)
    spectrum, grid_later, channel_mix = lax.optimization_barrier(
        (spectrum, grid_field, channel_mix)
    )
    arrived = lax.all_to_all(spectrum, both, split_axis=0, concat_axis=0, tiled=True)
    legendre = legendre_table(lax.axis_index(both))
    weight = mix_weight(channel_mix)
    pieces = grid_later.transpose(0, 2, 1).reshape(8, 8, 48, 128).transpose(1, 0, 2, 3)
    grids = [lax.dynamic_index_in_dim(pieces, place ^ k, 0, keepdims=False) for k in range(8)]
    grids = [grids[0]] + [
        lax.ppermute(grids[k], "chan", [(i, i ^ k) for i in range(8)]) for k in range(1, 8)
    ]
    places = jnp.arange(8, dtype=jnp.int32) ^ place
    field = mix_and_return(unpack_rows(arrived), legendre, degree_gain, weight, rows)
    returned = lax.all_to_all(
        pack_rows(field), both, split_axis=0, concat_axis=0, tiled=True
    )
    table = jnp.asarray(inverse_dft)
    grid = gather(places, table, grids)
    block_out = restore(unpack_rows(returned), table, grid)
    return block_out.transpose(0, 2, 1)


def solution(mesh):
    return jax.shard_map(
        on_device,
        mesh=mesh,
        in_specs=(P("lat", "chan", None), P(), P(), P()),
        out_specs=P("lat", None, "chan"),
        check_vma=False,
    )
```

```python
import math

import jax
import jax.numpy as jnp
import numpy as np
from jax import lax
from jax.experimental import pallas as pl
from jax.experimental.pallas import tpu as pltpu
from jax.sharding import PartitionSpec as P

NLAT = 512
EMBED = 384
NLON = 1024
DEGREES = 512
MODES = 512
VMEM_LIMIT = 20 * 1024 * 1024
WIDE_ROWS = 3072 + 64


def grid_points():
    theta = math.pi * (np.arange(NLAT, dtype=np.float64) + 0.5) / NLAT
    harmonic = np.arange(1, NLAT // 2 + 1, dtype=np.float64)
    series = np.sum(
        np.cos(2.0 * harmonic[None, :] * theta[:, None]) / (4.0 * harmonic * harmonic - 1.0),
        axis=1,
    )
    weights = 2.0 / NLAT * (1.0 - 2.0 * series)
    return theta, weights


def order_starts():
    return np.array(
        [
            0.5 * (math.lgamma(m + 1.5) - math.lgamma(1.5) - math.lgamma(m + 1.0) - math.log(2.0))
            / math.log(2.0)
            for m in range(MODES)
        ]
    )


def dft_tables():
    phase = np.arange(MODES)[:, None] * np.arange(NLON)[None, :] % NLON
    angle = 2.0 * math.pi / NLON * phase
    parts = np.stack([np.cos(angle), -np.sin(angle)], axis=1)
    factor = np.where(np.arange(MODES) == 0, 1.0, 2.0)[:, None, None]
    forward = (parts / NLON).reshape(2, MODES // 2, 2, NLON).transpose(0, 2, 1, 3)
    forward = forward.reshape(2 * MODES, NLON)
    inverse = (parts * factor).transpose(1, 0, 2).reshape(2 * MODES, NLON)
    return forward.astype(jnp.bfloat16), inverse.astype(jnp.bfloat16)


def pair_weight(channel_mix):
    real_part = channel_mix[0]
    imag_part = channel_mix[1]
    upper = jnp.concatenate([real_part, imag_part], axis=1)
    lower = jnp.concatenate([-imag_part, real_part], axis=1)
    return jnp.concatenate([upper, lower], axis=0)


def permuted_latitudes():
    high, a, low = np.meshgrid(np.arange(4), np.arange(8), np.arange(16), indexing="ij")
    return ((16 * high + low) * 8 + a).reshape(-1)


def hold_kernel(table_ref, out_ref):
    out_ref[...] = table_ref[...]


def hold(table):
    vmem = pl.BlockSpec(memory_space=pltpu.VMEM)
    return pl.pallas_call(
        hold_kernel,
        out_shape=jax.ShapeDtypeStruct(table.shape, table.dtype),
        in_specs=[vmem],
        out_specs=vmem,
        cost_estimate=pl.CostEstimate(flops=0, bytes_accessed=4_000_000, transcendentals=0),
        compiler_params=pltpu.CompilerParams(vmem_limit_bytes=VMEM_LIMIT),
    )(table)


def transform_kernel(
    weights_ref, grid_ref, gain_ref, table_ref, out_ref, normed_ref, wide_ref, narrow_ref, out_sems
):
    row = lax.axis_index("lat") * 8 + lax.axis_index("chan")
    spot = lax.broadcasted_iota(jnp.int32, (4, 128), 0) * 128
    spot = spot + lax.broadcasted_iota(jnp.int32, (4, 128), 1)
    share = jnp.sum(jnp.where(spot == row, weights_ref[...], 0.0), axis=1, keepdims=True)
    share = jnp.sum(share, axis=0, keepdims=True)
    gain = gain_ref[...]
    sums = [None, None]
    for part in range(2):
        for piece in range(4):
            rows = slice(512 * part + 128 * piece, 512 * part + 128 * piece + 128)
            values = grid_ref[rows, :].astype(jnp.float32)
            mean_value = jnp.mean(values, axis=1, keepdims=True)
            centered = values - mean_value
            variance = jnp.mean(centered * centered, axis=1, keepdims=True)
            normed_ref[rows, :] = (centered * lax.rsqrt(variance + 1e-05) * gain).astype(
                jnp.bfloat16
            )
        for half in range(2):
            term = jnp.dot(
                table_ref[512 * half : 512 * half + 512, 512 * part : 512 * part + 512],
                normed_ref[512 * part : 512 * part + 512, :],
                preferred_element_type=jnp.float32,
            )
            sums[half] = term if part == 0 else sums[half] + term
    results = []
    for half in range(2):
        spectrum = sums[half] * share
        first = 1536 * half
        for r in range(2):
            for t in range(3):
                wide_ref[pl.ds(first + 2 * t + r, 256, stride=6), :] = spectrum[
                    256 * r : 256 * r + 256, 128 * t : 128 * t + 128
                ]
        rows = slice(first, first + 1536)
        narrow_ref[rows, :] = wide_ref[rows, :].astype(jnp.bfloat16)
        results.append(
            pltpu.make_async_copy(narrow_ref.at[rows], out_ref.at[rows], out_sems.at[half])
        )
        results[half].start()
    for half in range(2):
        results[half].wait()


def transform(weights, grid, gain, table):
    vmem = pl.BlockSpec(memory_space=pltpu.VMEM)
    return pl.pallas_call(
        transform_kernel,
        out_shape=jax.ShapeDtypeStruct((6 * MODES, 128), jnp.bfloat16),
        in_specs=[vmem] * 4,
        out_specs=pl.BlockSpec(memory_space=pltpu.MemorySpace.HBM),
        scratch_shapes=[
            pltpu.VMEM((NLON, EMBED), jnp.bfloat16),
            pltpu.VMEM((WIDE_ROWS, 128), jnp.float32),
            pltpu.VMEM((6 * MODES, 128), jnp.bfloat16),
            pltpu.SemaphoreType.DMA((2,)),
        ],
        cost_estimate=pl.CostEstimate(
            flops=800_000_000, bytes_accessed=4_000_000, transcendentals=1024
        ),
        compiler_params=pltpu.CompilerParams(vmem_limit_bytes=VMEM_LIMIT),
    )(weights, grid, gain, table)


def spread_rows(source_ref, wide_ref, pieces_ref):
    wide_ref[0:3072, :] = source_ref[...].astype(jnp.float32)
    for r in range(2):
        for t in range(3):
            pieces_ref[512 * r : 512 * r + 512, 128 * t : 128 * t + 128] = wide_ref[
                pl.ds(2 * t + r, 512, stride=6), :
            ].astype(jnp.bfloat16)


def pack_rows(rows):
    return rows.reshape(512, 3, 2, 128).transpose(0, 2, 1, 3).reshape(512, 2, EMBED)


def unpack_rows(pieces):
    return pieces.reshape(512, 2, 3, 128).transpose(0, 2, 1, 3).reshape(3072, 128)


def legendre_kernel(coef_ref, cos_ref, start_ref, exponent_ref, table_ref):
    cos_row = cos_ref[...]
    start = start_ref[...]

    def block(index, state):
        one, two, power = state
        base = index * 16
        parts = []
        for half in range(2):
            rows = []
            for k in range(8):
                level = base + 8 * half + k
                a = coef_ref[0, level]
                b = coef_ref[1, level]
                s = coef_ref[2, level]
                one, two = (a * cos_row) * one - b * two + s * start, one
                rows.append(one)
            parts.append(jnp.concatenate(rows, axis=0) * jnp.exp2(power))
            large = jnp.abs(one) > 1000.0
            factor = jnp.where(large, 2.0**-40, 1.0)
            power = power + jnp.where(large, 40.0, 0.0)
            one, two = one * factor, two * factor
        here = pl.ds(pl.multiple_of(base, 16), 16)
        table_ref[here, :] = jnp.concatenate(parts, axis=0).astype(jnp.bfloat16)
        return one, two, power

    zeros = jnp.zeros((1, NLAT), jnp.float32)
    lax.fori_loop(0, DEGREES // 16, block, (zeros, zeros, exponent_ref[...]))


def legendre_table(order):
    theta_row = grid_points()[0][permuted_latitudes()].reshape(1, NLAT)
    cos_row = jnp.asarray(np.cos(theta_row), jnp.float32)
    log_sine = jnp.asarray(np.log2(np.sin(theta_row)), jnp.float32)
    starts = jnp.asarray(order_starts(), jnp.float32)
    start = jnp.sum(jnp.where(jnp.arange(MODES) == order, starts, 0.0))
    m = order.astype(jnp.float32)
    log_start = start + m * log_sine
    exponent = jnp.floor(log_start)
    mantissa = jnp.exp2(log_start - exponent)
    level = jnp.arange(DEGREES, dtype=jnp.float32)
    denom = jnp.maximum(level * level - m * m, 1.0)
    above = level > m
    coef_a = jnp.where(above, jnp.sqrt(jnp.maximum(4.0 * level * level - 1.0, 1.0) / denom), 0.0)
    coef_b = jnp.sqrt(
        jnp.maximum((level - 1.0) * (level - 1.0) - m * m, 0.0)
        * (2.0 * level + 1.0)
        / (denom * jnp.maximum(2.0 * level - 3.0, 1.0))
    )
    coef_b = jnp.where(above, coef_b, 0.0)
    first = jnp.where(level == m, 1.0, 0.0)
    coefs = jnp.stack([coef_a, coef_b, first])
    vmem = pl.BlockSpec(memory_space=pltpu.VMEM)
    return pl.pallas_call(
        legendre_kernel,
        out_shape=jax.ShapeDtypeStruct((DEGREES, NLAT), jnp.bfloat16),
        in_specs=[pl.BlockSpec(memory_space=pltpu.SMEM)] + [vmem] * 3,
        out_specs=vmem,
        cost_estimate=pl.CostEstimate(
            flops=40_000_000, bytes_accessed=8_000_000, transcendentals=65536
        ),
        compiler_params=pltpu.CompilerParams(vmem_limit_bytes=VMEM_LIMIT),
    )(coefs, cos_row, mantissa, exponent)


def mix_kernel(
    arrived_ref,
    table_ref,
    gain_ref,
    weight_ref,
    spare_ref,
    out_ref,
    wide_ref,
    pieces_ref,
    field_ref,
    narrow_ref,
    out_sems,
):
    wide_ref[0:3072, :] = arrived_ref[...].astype(jnp.float32)
    for r in range(2):
        for high in range(4):
            for a in range(8):
                rows = slice(128 * high + 16 * a, 128 * high + 16 * a + 16)
                for t in range(3):
                    first = 768 * high + 6 * a + 2 * t + r
                    columns = slice(384 * r + 128 * t, 384 * r + 128 * t + 128)
                    pieces_ref[rows, columns] = wide_ref[
                        pl.ds(first, 16, stride=48), :
                    ].astype(jnp.bfloat16)
    gain = gain_ref[...]
    coeffs = jnp.dot(table_ref[...], pieces_ref[...], preferred_element_type=jnp.float32)
    scaled = (coeffs * jnp.concatenate([gain, gain], axis=1)).astype(jnp.bfloat16)
    mixed = lax.dot_general(
        weight_ref[...], scaled, (((1,), (1,)), ((), ())), preferred_element_type=jnp.float32
    ).astype(jnp.bfloat16)
    lane = lax.broadcasted_iota(jnp.int32, (8, 128), 1)
    masks = {d: (lane & d) != 0 for d in (1, 2, 4, 8)}
    results = []
    for pair in range(2):
        field_ref[:, 256 * pair : 256 * pair + 256] = jnp.dot(
            mixed, table_ref[:, 256 * pair : 256 * pair + 256], preferred_element_type=jnp.float32
        )
    for high in range(4):
        columns = slice(128 * high, 128 * high + 128)

        def group(index, carry, high=high, columns=columns):
            rows = index * 16
            halves = []
            for half in range(2):
                pieces = []
                for i in range(16):
                    piece = field_ref[pl.ds(48 * i + rows + 8 * half, 8), columns]
                    pieces.append(pltpu.roll(piece, i, 1) if i else piece)
                for d in (1, 2, 4, 8):
                    pieces = [
                        jnp.where(masks[d], pieces[(k + d) % 16], pieces[k]) for k in range(16)
                    ]
                halves.append([pieces[(16 - low) % 16] for low in range(16)])
            for low in range(16):
                both = jnp.concatenate([halves[0][low], halves[1][low]], axis=0)
                here = pl.ds(48 * (high * 16 + low) + rows, 16)
                narrow_ref[here, :] = both.astype(jnp.bfloat16)
            return carry

        for index in range(3):
            group(index, 0)
        here = slice(768 * high, 768 * high + 768)
        results.append(
            pltpu.make_async_copy(narrow_ref.at[here], out_ref.at[here], out_sems.at[high])
        )
        results[high].start()
    for high in range(4):
        results[high].wait()


def mix_and_return(arrived, table, gain, weight, spare):
    vmem = pl.BlockSpec(memory_space=pltpu.VMEM)
    return pl.pallas_call(
        mix_kernel,
        out_shape=jax.ShapeDtypeStruct((6 * MODES, 128), jnp.bfloat16),
        in_specs=[vmem] * 4 + [pl.BlockSpec(memory_space=pltpu.MemorySpace.HBM)],
        out_specs=pl.BlockSpec(memory_space=pltpu.MemorySpace.HBM),
        input_output_aliases={4: 0},
        scratch_shapes=[
            pltpu.VMEM((WIDE_ROWS, 128), jnp.float32),
            pltpu.VMEM((NLAT, 2 * EMBED), jnp.bfloat16),
            pltpu.VMEM((2 * EMBED, NLAT), jnp.float32),
            pltpu.VMEM((6 * MODES, 128), jnp.bfloat16),
            pltpu.SemaphoreType.DMA((4,)),
        ],
        cost_estimate=pl.CostEstimate(
            flops=1_400_000_000, bytes_accessed=4_000_000, transcendentals=0
        ),
        compiler_params=pltpu.CompilerParams(vmem_limit_bytes=VMEM_LIMIT),
    )(arrived, table, gain, weight, spare)


def gather_kernel(place_ref, table_ref, *refs):
    grid_refs, out_ref = refs[:8], refs[8]
    for k in range(8):
        columns = pl.ds(pl.multiple_of(place_ref[k] * 128, 128), 128)
        out_ref[:, :, columns] = grid_refs[k][...]


def gather(places, table, grids):
    vmem = pl.BlockSpec(memory_space=pltpu.VMEM)
    return pl.pallas_call(
        gather_kernel,
        out_shape=jax.ShapeDtypeStruct((8, 48, NLON), jnp.bfloat16),
        in_specs=[pl.BlockSpec(memory_space=pltpu.SMEM)] + [vmem] * 9,
        out_specs=vmem,
        cost_estimate=pl.CostEstimate(flops=0, bytes_accessed=6_000_000, transcendentals=0),
        compiler_params=pltpu.CompilerParams(vmem_limit_bytes=VMEM_LIMIT),
    )(places, table, *grids)


def restore_kernel(
    spectrum_ref,
    table_ref,
    grid_ref,
    out_ref,
    wide_ref,
    pieces_ref,
    field_ref,
    held_ref,
    narrow_ref,
    grid_sem,
    out_sems,
):
    grid_copy = pltpu.make_async_copy(grid_ref, held_ref, grid_sem)
    grid_copy.start()
    spread_rows(spectrum_ref, wide_ref, pieces_ref)
    turned = pieces_ref[...].T
    field = jnp.dot(turned, table_ref[...], preferred_element_type=jnp.float32)
    for t in range(3):
        for s in range(8):
            columns = slice(128 * s, 128 * s + 128)
            field_ref[pl.ds(1152 * t + s, 128, stride=8), :] = field[128 * t : 128 * t + 128, columns]
            field_ref[pl.ds(1152 * t + 1024 + s, 16, stride=8), :] = field[
                128 * t : 128 * t + 16, columns
            ]
    turn = pl.multiple_of(lax.rem(lax.axis_index("lat"), 16) * 8, 8)
    grid_copy.wait()
    results = []
    for a in range(8):
        for t in range(3):
            first = 8 * (144 * t + 16 * a)
            piece = jnp.concatenate(
                [field_ref[pl.ds(first + turn + s, 16, stride=8), :] for s in range(8)], axis=1
            )
            rows = slice(16 * t, 16 * t + 16)
            own = held_ref[a, rows, :].astype(jnp.float32)
            narrow_ref[a, rows, :] = (own + piece).astype(jnp.bfloat16)
        results.append(pltpu.make_async_copy(narrow_ref.at[a], out_ref.at[a], out_sems.at[a]))
        results[a].start()
    for a in range(8):
        results[a].wait()


def restore(spectrum, table, grid):
    vmem = pl.BlockSpec(memory_space=pltpu.VMEM)
    return pl.pallas_call(
        restore_kernel,
        out_shape=jax.ShapeDtypeStruct((8, 48, NLON), jnp.bfloat16),
        in_specs=[vmem, vmem, pl.BlockSpec(memory_space=pltpu.MemorySpace.HBM)],
        out_specs=pl.BlockSpec(memory_space=pltpu.MemorySpace.HBM),
        input_output_aliases={2: 0},
        scratch_shapes=[
            pltpu.VMEM((WIDE_ROWS, 128), jnp.float32),
            pltpu.VMEM((2 * MODES, EMBED), jnp.bfloat16),
            pltpu.VMEM((3 * 144 * 8, 128), jnp.float32),
            pltpu.VMEM((8, 48, NLON), jnp.bfloat16),
            pltpu.VMEM((8, 48, NLON), jnp.bfloat16),
            pltpu.SemaphoreType.DMA,
            pltpu.SemaphoreType.DMA((8,)),
        ],
        cost_estimate=pl.CostEstimate(
            flops=800_000_000, bytes_accessed=4_000_000, transcendentals=0
        ),
        compiler_params=pltpu.CompilerParams(vmem_limit_bytes=VMEM_LIMIT),
    )(spectrum, table, grid)


def mix_weight(channel_mix):
    paired = pair_weight(channel_mix).T.reshape(2, 24, 16, 2 * EMBED)
    return paired.transpose(2, 1, 0, 3).reshape(2 * EMBED, 2 * EMBED)


def on_device(grid_field, norm_gain, degree_gain, channel_mix):
    both = ("lat", "chan")
    place = lax.axis_index("chan")
    forward_dft, inverse_dft = dft_tables()
    own = lax.all_to_all(grid_field, "chan", split_axis=0, concat_axis=0, tiled=True)
    own = own.reshape(NLON, EMBED)
    weights = jnp.asarray(grid_points()[1].reshape(4, 128), jnp.float32)
    own, forward_dft = lax.optimization_barrier((own, hold(jnp.asarray(forward_dft))))
    rows = transform(weights, own, norm_gain.reshape(1, EMBED), forward_dft)
    spectrum = pack_rows(rows)
    spectrum, grid_later, channel_mix = lax.optimization_barrier(
        (spectrum, grid_field, channel_mix)
    )
    arrived = lax.all_to_all(spectrum, both, split_axis=0, concat_axis=0, tiled=True)
    legendre = legendre_table(lax.axis_index(both))
    weight = mix_weight(channel_mix)
    pieces = grid_later.transpose(0, 2, 1).reshape(8, 8, 48, 128).transpose(1, 0, 2, 3)
    grids = [lax.dynamic_index_in_dim(pieces, place ^ k, 0, keepdims=False) for k in range(8)]
    grids = [grids[0]] + [
        lax.ppermute(grids[k], "chan", [(i, i ^ k) for i in range(8)]) for k in range(1, 8)
    ]
    places = jnp.arange(8, dtype=jnp.int32) ^ place
    field = mix_and_return(unpack_rows(arrived), legendre, degree_gain, weight, rows)
    returned = lax.all_to_all(
        pack_rows(field), both, split_axis=0, concat_axis=0, tiled=True
    )
    table = jnp.asarray(inverse_dft)
    grid = gather(places, table, grids)
    block_out = restore(unpack_rows(returned), table, grid)
    return block_out.transpose(0, 2, 1)


def solution(mesh):
    return jax.shard_map(
        on_device,
        mesh=mesh,
        in_specs=(P("lat", "chan", None), P(), P(), P()),
        out_specs=P("lat", None, "chan"),
        check_vma=False,
    )
```
